32 devices in a mesh: rep: 4 (over y, x), ep: 8 (over z, core).
Axes of the slice: x: 2, y: 2, z: 4, core: 2. Of those that a mesh axis runs over, the one named last changes fastest.
Arguments:
- q_latent: bfloat16 [256, 128, 512], P(('rep', 'ep')), may hold values from -6 to 6
- q_rope: bfloat16 [256, 128, 64], P(('rep', 'ep')), may hold values from -104 to 104
- cache_latent: bfloat16 [256, 128, 512], P(('rep', 'ep')), may hold values from -6 to 6
- cache_rope: bfloat16 [256, 128, 64], P(('rep', 'ep')), may hold values from -6 to 6
- cache_len: int32 [256], P(('rep', 'ep')), may hold values from 32 to 128, as said below
- stream: bfloat16 [256, 7168], P(('rep', 'ep')), may hold values from -6 to 6
- norm_gain: float32 [7168], replicated, may hold values from 0.1 to 1.9
- expert_ids: int32 [256, 8], P(('rep', 'ep')), may hold values from 0 to 15, all different within a row; in each aligned block of 8 rows (0 to 7, 8 to 15, ...) at most 8 rows name the same one
- route_weights: bfloat16 [256, 8], P(('rep', 'ep')), may hold values from 0.099609375 to 1
- w_gate: bfloat16 [16, 7168, 1024], P('ep', None, 'rep'), may hold values from -0.0625 to 0.0625
- w_up: bfloat16 [16, 7168, 1024], P('ep', None, 'rep'), may hold values from -0.0625 to 0.0625
- w_down: bfloat16 [16, 1024, 7168], P('ep', 'rep'), may hold values from -0.1875 to 0.1875
Outputs:
- attn_latent: bfloat16 [256, 128, 512], P(('rep', 'ep'))
- layer_out: bfloat16 [256, 7168], P(('rep', 'ep'))
The draws below stay inside these ranges and needn't reach their ends.
Inputs may be any that keep to these rules, and one draw needn't show every extreme that they name: `expert_ids`: each row names 8 different experts; within the rows of one device no expert is named by more than 8 rows, a bound that some block reaches. `cache_len`: some row has all 128 positions live.
All inputs are finite; a program needn't handle non-finite values.
Results may differ from the reference program's by a relative error of at most 0.01.
Values may be sent and summed in bfloat16 or wider, within the bound.
A program may use at most 128 MiB of HBM per device.

```python
import math
import jax
import jax.numpy as jnp
import numpy as np
from jax import lax

D = 7168
HEADS = 128
LATENT = 512
ROPE = 64
FF = 1024
TOP = 8
R_DEV = 8
CACHE = 128
EXPERTS = 16
ROWS = 256
CAP = 8
N_REP = 4
N_EP = 8


def attention_draws(key):
    key_ql = jax.random.fold_in(key, 101)
    key_qr = jax.random.fold_in(key, 102)
    key_cl = jax.random.fold_in(key, 103)
    key_cr = jax.random.fold_in(key, 104)
    query_lat = jnp.clip(jax.random.normal(key_ql, (ROWS, HEADS, LATENT), jnp.float32), -6.0, 6.0)
    query_rot = jnp.clip(jax.random.normal(key_qr, (ROWS, HEADS, ROPE), jnp.float32), -6.0, 6.0)
    keys_lat = jnp.clip(jax.random.normal(key_cl, (ROWS, CACHE, LATENT), jnp.float32), -6.0, 6.0)
    keys_rot = jnp.clip(jax.random.normal(key_cr, (ROWS, CACHE, ROPE), jnp.float32), -6.0, 6.0)
    return (query_lat, query_rot, keys_lat, keys_rot)


def draw_q_latent(key, part):
    return attention_draws(key)[0].astype(jnp.bfloat16)


def draw_q_rope(key, part):
    return attention_draws(key)[1].astype(jnp.bfloat16)


def draw_cache_latent(key, part):
    return attention_draws(key)[2].astype(jnp.bfloat16)


def draw_cache_rope(key, part):
    return attention_draws(key)[3].astype(jnp.bfloat16)


def draw_cache_len(key, part):
    lengths = jax.random.randint(jax.random.fold_in(key, 201), (ROWS,), CACHE // 4, CACHE + 1, jnp.int32)
    return lengths.at[0].set(CACHE)


def levels(key, shape, shards, least, high):
    factor_of = 1.0
    for dim, blocks in shards:
        steps = jax.random.uniform(jax.random.fold_in(jax.random.fold_in(key, 6), dim), (blocks,), jnp.float32, least / len(shards), high / len(shards))
        factor_of = factor_of * jnp.repeat(jnp.exp(steps), shape[dim] // blocks).reshape((-1,) + (1,) * (len(shape) - 1 - dim))
    return factor_of


def shared_out(own_key, own, number, rows, count, top, reach, lean):
    order = jax.random.permutation(own_key, count)
    crowded, ordinary = load_shares(count, rows * top, reach, lean, True), load_shares(count, rows * top, reach, lean, False)
    places = jnp.arange(count)

    def named(tallies, turn):
        used = int((tallies > 0).sum())
        fixed = max(1, used // 4)
        shifted = fixed + (places - fixed + turn * (used - fixed)) % max(1, count - fixed)
        return jnp.zeros((count,), jnp.int32).at[order[jnp.where(places < fixed, places, shifted)]].set(jnp.asarray(tallies, jnp.int32))

    tallies = jnp.where(number % 4 == 0, named(crowded, number // 4), named(ordinary, number - number // 4 - 1))
    mixed = jax.random.permutation(jax.random.fold_in(own, 3), count)
    donor, receiver = mixed[0:count // 2 * 2:2], mixed[1:count // 2 * 2:2]
    slack = jnp.minimum(tallies[donor] - 1, reach - tallies[receiver]) // 2
    slack = jnp.where((donor == order[0]) | (receiver == order[0]) | (tallies[receiver] == 0), 0, jnp.maximum(slack, 0))
    shifted = jax.random.randint(jax.random.fold_in(own, 4), (count // 2,), 0, 1 << 20) % (slack + 1)
    tallies = tallies.at[donor].add(-shifted).at[receiver].add(shifted)
    items = jnp.searchsorted(jnp.cumsum(tallies), jnp.arange(rows * top), side="right").astype(jnp.int32)
    grid = items.reshape(top, rows).T
    grid = grid[jax.random.permutation(jax.random.fold_in(own, 1), rows)]
    turn = jax.random.randint(jax.random.fold_in(own, 2), (rows, 1), 0, top)
    return jnp.take_along_axis(grid, (jnp.arange(top)[None, :] + turn) % top, axis=1)


def load_shares(number_of, total, most, skew, full):
    loads = [(1 << 20) // math.isqrt(standing ** skew) + 1 for standing in range(1, number_of + 1)]
    largest = most if full else min(most, max(-(-total // number_of), total * loads[0] // sum(loads)))
    least = 1 if total - largest >= number_of - 1 else 0
    counts, spare = [largest] + [least] * (number_of - 1), total - largest - least * (number_of - 1)
    while spare > 0:
        movable = [i for i in range(1, number_of) if counts[i] < largest] or [i for i in range(1, number_of) if counts[i] < most]
        whole, remaining = sum([loads[i] for i in movable]), spare
        for i in movable:
            extra = min(most - counts[i], max(1, remaining * loads[i] // whole), spare)
            counts[i] = counts[i] + extra
            spare = spare - extra
    return np.array(counts)


def gaussian(stream_key, dims, scale, most, split=(), kind=jnp.bfloat16):
    level = levels(stream_key, dims, split, -0.22, 0.18) if split else 1.0
    array = jax.random.normal(stream_key, dims, jnp.float32) * scale * level
    return jnp.minimum(jnp.maximum(array, -most), most).astype(kind)


def setup_inputs(seed: int = 0) -> dict:
    key_list = jax.random.split(jax.random.key(seed), 13)
    q_latent = draw_q_latent(jax.random.fold_in(key_list[12], 71), 0)
    q_rope = draw_q_rope(jax.random.fold_in(key_list[12], 71), 0)
    cache_latent = draw_cache_latent(jax.random.fold_in(key_list[12], 71), 0)
    cache_rope = draw_cache_rope(jax.random.fold_in(key_list[12], 71), 0)
    cache_len = draw_cache_len(jax.random.fold_in(key_list[12], 71), 0)
    stream = gaussian(key_list[5], (ROWS, D), 1.0, 6.0, ((0, 32),))
    norm_gain = jnp.clip(1.0 + 0.18 * jax.random.normal(key_list[6], (D,), jnp.float32), 0.1, 1.9)
    expert_ids_keys = jax.random.split(jax.random.fold_in(key_list[7], 1), ROWS // R_DEV)
    expert_ids_turns = jax.random.permutation(jax.random.fold_in(key_list[7], 3), ROWS // R_DEV)
    expert_ids = jax.vmap(lambda own, number: shared_out(jax.random.fold_in(key_list[7], 2), own, number, R_DEV, EXPERTS, TOP, CAP, 2))(expert_ids_keys, expert_ids_turns).reshape((ROWS, TOP))
    route_weights = jnp.clip(0.099609375 + 0.9003906 * jax.random.uniform(key_list[8], (ROWS, TOP), jnp.float32) ** levels(key_list[8], (ROWS, TOP), ((0, 32),), -0.2, 0.2), 0.099609375, 1.0).astype(jnp.bfloat16)
    w_gate = gaussian(key_list[9], (EXPERTS, D, FF), D ** -0.5, 0.0625, ((0, 8), (2, 4)))
    w_up = gaussian(key_list[10], (EXPERTS, D, FF), D ** -0.5, 0.0625, ((0, 8), (2, 4)))
    w_down = gaussian(key_list[11], (EXPERTS, FF, D), FF ** -0.5, 0.1875, ((0, 8), (1, 4)))
    return {"q_latent": q_latent, "q_rope": q_rope, "cache_latent": cache_latent, "cache_rope": cache_rope, "cache_len": cache_len, "stream": stream, "norm_gain": norm_gain, "expert_ids": expert_ids, "route_weights": route_weights, "w_gate": w_gate, "w_up": w_up, "w_down": w_down}


score_scale = 192.0 ** (-0.5)
norm_eps = 1e-06

def attend_row(item):
    query_lat, query_rot, keys_lat, keys_rot, length = item
    scores = (jnp.einsum('hl,tl->ht', query_lat.astype(jnp.float32), keys_lat.astype(jnp.float32)) + jnp.einsum('hr,tr->ht', query_rot.astype(jnp.float32), keys_rot.astype(jnp.float32))) * score_scale
    valid_mask = (jnp.arange(CACHE, dtype=jnp.int32) < length)[None, :]
    scores = jnp.where(valid_mask, scores, -1e+30)
    top_score = lax.optimization_barrier(jnp.max(scores, axis=-1, keepdims=True))
    exponent = jnp.where(valid_mask, jnp.exp(scores - top_score), 0.0)
    attn_weights = (exponent / lax.optimization_barrier(jnp.sum(exponent, axis=-1, keepdims=True))).astype(jnp.bfloat16)
    return jnp.einsum('ht,tl->hl', attn_weights.astype(jnp.float32), keys_lat.astype(jnp.float32)).astype(jnp.bfloat16)

def reference(q_latent, q_rope, cache_latent, cache_rope, cache_len, stream, norm_gain, expert_ids, route_weights, w_gate, w_up, w_down):
    attn_latent = lax.map(attend_row, (q_latent, q_rope, cache_latent, cache_rope, cache_len))
    stream_f = stream.astype(jnp.float32)
    normed = (stream_f * lax.rsqrt(lax.optimization_barrier(jnp.mean(stream_f * stream_f, axis=-1, keepdims=True)) + norm_eps) * norm_gain).astype(jnp.bfloat16)
    assigned = expert_ids.reshape(-1)
    onehot = (assigned[:, None] == jnp.arange(EXPERTS, dtype=jnp.int32)[None, :]).astype(jnp.int32)
    earlier = jnp.cumsum(onehot, axis=0) - onehot
    position = lax.optimization_barrier(jnp.sum(earlier * onehot, axis=-1)).astype(jnp.int32)
    slot_limit = N_REP * N_EP * CAP
    row_of = (jnp.arange(ROWS * TOP, dtype=jnp.int32) // TOP).astype(jnp.int32)
    table = jnp.zeros((EXPERTS, slot_limit), jnp.int32).at[assigned, position].set(row_of)
    weight_table = jnp.zeros((EXPERTS, slot_limit), jnp.float32).at[assigned, position].set(route_weights.reshape(-1).astype(jnp.float32))
    block = FF // N_REP

    def expert_step(total, item):
        gate_mat, up_mat, down_mat, index_row, weight_row = item
        rows_in = normed[index_row]
        summed = jnp.zeros((slot_limit, D), jnp.float32)
        for quarter in range(N_REP):
            lower = quarter * block
            gate_act = jnp.dot(rows_in, gate_mat[:, lower:lower + block], preferred_element_type=jnp.float32)
            up_act = jnp.dot(rows_in, up_mat[:, lower:lower + block], preferred_element_type=jnp.float32)
            hidden = (jax.nn.silu(gate_act) * up_act).astype(jnp.bfloat16)
            piece = jnp.dot(hidden, down_mat[lower:lower + block, :], preferred_element_type=jnp.float32).astype(jnp.bfloat16)
            piece = lax.optimization_barrier(piece)
            summed = summed + piece.astype(jnp.float32)
        total = total.at[index_row].add(weight_row[:, None] * summed)
        return (total, None)
    expert_sum = lax.scan(expert_step, jnp.zeros((ROWS, D), jnp.float32), (w_gate, w_up, w_down, table, weight_table))[0]
    layer_out = (stream_f + expert_sum).astype(jnp.bfloat16)
    return (attn_latent, layer_out)
```

```python
import functools

import jax
import jax.numpy as jnp
from jax import lax
from jax.experimental import pallas as pl
from jax.experimental.pallas import tpu as pltpu
from jax.sharding import PartitionSpec as P

MESH = pl.DeviceIdType.MESH
LANES = 128
PARTS = 7

score_scale = 192.0 ** (-0.5)
norm_eps = 1e-06


def slot_ranks(routes):
    order = jnp.arange(routes.shape[0], dtype=jnp.int32)
    earlier = (routes[:, None] == routes[None, :]) & (order[None, :] < order[:, None])
    return jnp.sum(earlier.astype(jnp.int32), axis=-1)


def fill_slots(features, slot_index, row_index, slot_total):
    sources = jnp.zeros((slot_total,), jnp.int32).at[slot_index].set(row_index)
    filled = jnp.zeros((slot_total,), features.dtype).at[slot_index].set(1)
    return features[sources] * filled[:, None]


def expert_block(tokens_in, gate_part, up_part, down_part):
    gate_act = jnp.dot(tokens_in, gate_part, preferred_element_type=jnp.float32)
    up_act = jnp.dot(tokens_in, up_part, preferred_element_type=jnp.float32)
    hidden = (jax.nn.silu(gate_act) * up_act).astype(jnp.bfloat16)
    return jnp.dot(hidden, down_part, preferred_element_type=jnp.float32).astype(jnp.bfloat16)


def per_device(
    q_latent,
    q_rope,
    cache_latent,
    cache_rope,
    cache_len,
    stream,
    norm_gain,
    expert_ids,
    route_weights,
    w_gate,
    w_up,
    w_down,
):
    ep_count = lax.axis_size("ep")
    row_count, feature_dim = stream.shape
    local_count = w_gate.shape[0]
    top_count = expert_ids.shape[1]
    expert_total = local_count * ep_count
    capacity = max(2, 2 * row_count * top_count // expert_total)
    stream_f = stream.astype(jnp.float32)
    normed = (
        stream_f
        * lax.rsqrt(jnp.mean(stream_f * stream_f, axis=-1, keepdims=True) + norm_eps)
        * norm_gain
    ).astype(jnp.bfloat16)
    flat_routes = expert_ids.reshape(-1)
    rank_in = slot_ranks(flat_routes)
    expert_slot = flat_routes % local_count * ep_count + flat_routes // local_count
    slot_index = expert_slot * capacity + rank_in
    row_index = jnp.arange(row_count * top_count, dtype=jnp.int32) // top_count
    slot_total = expert_total * capacity
    outgoing = fill_slots(normed, slot_index, row_index, slot_total).reshape(
        local_count, ep_count, capacity, feature_dim
    )
    incoming = lax.all_to_all(outgoing, "ep", split_axis=1, concat_axis=1, tiled=True)
    incoming = incoming.reshape(local_count, ep_count * capacity, feature_dim)
    scores = (
        jnp.einsum("ihl,itl->iht", q_latent, cache_latent, preferred_element_type=jnp.float32)
        + jnp.einsum("ihr,itr->iht", q_rope, cache_rope, preferred_element_type=jnp.float32)
    ) * score_scale
    valid_mask = (
        jnp.arange(cache_latent.shape[1], dtype=jnp.int32)[None, None, :] < cache_len[:, None, None]
    )
    scores = jnp.where(valid_mask, scores, -1e30)
    top_score = jnp.max(scores, axis=-1, keepdims=True)
    exponent = jnp.where(valid_mask, jnp.exp(scores - top_score), 0.0)
    attn_weights = (exponent / jnp.sum(exponent, axis=-1, keepdims=True)).astype(jnp.bfloat16)
    attn_latent = jnp.einsum(
        "iht,itl->ihl", attn_weights, cache_latent, preferred_element_type=jnp.float32
    ).astype(jnp.bfloat16)
    everyone = lax.all_gather(incoming, "rep", axis=1, tiled=True)
    partials = jax.vmap(expert_block)(everyone, w_gate, w_up, w_down)
    partials = lax.optimization_barrier(partials)
    summed = lax.psum_scatter(
        partials.astype(jnp.float32).astype(jnp.bfloat16), "rep", scatter_dimension=1, tiled=True
    ).astype(jnp.float32)
    returned = lax.all_to_all(
        summed.reshape(local_count, ep_count, capacity, feature_dim).astype(jnp.bfloat16),
        "ep",
        split_axis=1,
        concat_axis=1,
        tiled=True,
    ).astype(jnp.float32)
    picked = returned.reshape(slot_total, feature_dim)[slot_index].reshape(
        row_count, top_count, feature_dim
    )
    expert_sum = jnp.einsum(
        "rk,rkd->rd", route_weights.astype(jnp.float32), picked, precision=lax.Precision.HIGHEST
    )
    layer_out = (stream_f + expert_sum).astype(jnp.bfloat16)
    return (attn_latent, layer_out)


def fused_kernel(
    parts,
    ql_hbm, qr_hbm, cl_hbm, cr_hbm, len_ref, stream_ref, gain_ref, ids_ref, rw_ref,
    wg_hbm, wu_hbm, wd_hbm,
    attn_hbm, out_ref,
    ql, qr, cl, cr, attn, wg, wu, wd,
    nrm, swap_out, swap_in, xs, table, acc, hid,
    ysib, yown, r1, zb, ra, rb, rc, fin, fin_in,
    load_sem, w_sem, swap_sem,
    gz_s, gz_r, gc_s, gc_r, gf_s, gf_r, gs_s, gs_r,
    r1_s, r1_r, ra_s, ra_r, rb_s, rb_r, rc_s, rc_r, fin_s, fin_r,
):
    rep = lax.axis_index("rep")
    ep = lax.axis_index("ep")
    z, c = ep // 2, ep % 2
    other = 1 - c
    xn = rep + 1 - 2 * (rep % 2)
    yn = (rep + 2) % 4
    dg = 3 - rep
    sib_id = (rep, z * 2 + other)
    x_id, y_id = (xn, ep), (yn, ep)

    def z_id(d):
        return (rep, ((z + d) % 4) * 2 + c)

    partners = [sib_id, x_id, y_id, z_id(1), z_id(2), z_id(3)]
    rows, width = stream_ref.shape
    half = width // 2
    chunk = half // parts
    local = wg.shape[0]
    ff = wg.shape[2]
    total = 32 * rows

    barrier = pltpu.get_barrier_semaphore()
    for p in partners:
        pl.semaphore_signal(barrier, inc=1, device_id=p, device_id_type=MESH)

    loads = []
    for n, (a, b) in enumerate([(ql_hbm, ql), (cl_hbm, cl), (qr_hbm, qr), (cr_hbm, cr)]):
        loads.append(pltpu.make_async_copy(a, b, load_sem.at[n]))
    weights = []
    for e in range(local):
        weights.append(pltpu.make_async_copy(wg_hbm.at[e], wg.at[e], w_sem.at[3 * e]))
        weights.append(pltpu.make_async_copy(wu_hbm.at[e], wu.at[e], w_sem.at[3 * e + 1]))
        weights.append(
            pltpu.make_async_copy(wd_hbm.at[e], wd.at[pl.ds(e * ff, ff)], w_sem.at[3 * e + 2])
        )
    for copy in loads + weights:
        copy.start()

    stream_f = stream_ref[...].astype(jnp.float32)
    scale = lax.rsqrt(jnp.mean(stream_f * stream_f, axis=-1, keepdims=True) + norm_eps)
    normed = (stream_f * scale * gain_ref[...]).astype(jnp.bfloat16).astype(jnp.float32)
    for h in range(2):
        nrm[h, :, :half] = normed[:, h * half : (h + 1) * half]
    lane = lax.broadcasted_iota(jnp.int32, (rows, LANES), 1)
    dense = jnp.zeros((rows, LANES), jnp.float32)
    ids, rw = ids_ref[...], rw_ref[...].astype(jnp.float32)
    for k in range(ids.shape[1]):
        dense = dense + jnp.where(lane == ids[:, k : k + 1], rw[:, k : k + 1], 0.0)
    for h in range(2):
        nrm[h, :, half:] = dense
    swap_out[...] = nrm[other]
    pl.semaphore_wait(barrier, len(partners))

    sent = []

    def send(src, dst, send_sem, recv_sem, to):
        copy = pltpu.make_async_remote_copy(
            src_ref=src, dst_ref=dst, send_sem=send_sem, recv_sem=recv_sem,
            device_id=to, device_id_type=MESH,
        )
        copy.start()
        sent.append(copy)

    def arrived(dst, send_sem, recv_sem, to):
        pltpu.make_async_remote_copy(
            src_ref=dst, dst_ref=dst, send_sem=send_sem, recv_sem=recv_sem,
            device_id=to, device_id_type=MESH,
        ).wait_recv()

    send(swap_out, swap_in, swap_sem.at[0], swap_sem.at[1], sib_id)
    arrived(swap_in, swap_sem.at[0], swap_sem.at[1], sib_id)
    mine, theirs = nrm[c], swap_in[...]
    both = jnp.where(
        c == 0,
        jnp.concatenate([mine, theirs], axis=0),
        jnp.concatenate([theirs, mine], axis=0),
    ).astype(jnp.bfloat16)
    table[rep, z] = both[:, half:]
    units = [table]
    for k in range(parts):
        xs[c * parts + k, rep, z] = both[:, k * chunk : (k + 1) * chunk]
        units.append(xs.at[c * parts + k])

    def gather_z(u):
        for d in (1, 2, 3):
            blk = units[u].at[rep, z]
            send(blk, blk, gz_s.at[u, d - 1], gz_r.at[u, d - 1], z_id(d))

    def gather_xy(u):
        for d in (1, 2, 3):
            blk = units[u].at[rep, (z + 4 - d) % 4]
            arrived(blk, gz_s.at[u, d - 1], gz_r.at[u, d - 1], z_id(4 - d))
        col = units[u].at[rep]
        send(col, col, gc_s.at[u, 0], gc_r.at[u, 0], x_id)
        send(col, col, gc_s.at[u, 1], gc_r.at[u, 1], y_id)

    def gather_diag(u):
        arrived(units[u].at[xn], gc_s.at[u, 0], gc_r.at[u, 0], x_id)
        low = units[u].at[xn, pl.ds(0, 2)]
        send(low, low, gf_s.at[u, 0], gf_r.at[u, 0], y_id)
        arrived(units[u].at[yn], gc_s.at[u, 1], gc_r.at[u, 1], y_id)
        high = units[u].at[yn, pl.ds(2, 2)]
        send(high, high, gf_s.at[u, 1], gf_r.at[u, 1], x_id)

    def gather_done(u):
        arrived(units[u].at[dg, pl.ds(0, 2)], gf_s.at[u, 0], gf_r.at[u, 0], y_id)
        arrived(units[u].at[dg, pl.ds(2, 2)], gf_s.at[u, 1], gf_r.at[u, 1], x_id)
        if u > 0:
            send(units[u], units[u], gs_s.at[u - 1], gs_r.at[u - 1], sib_id)

    def attend(i):
        dims = (((1,), (1,)), ((), ()))
        s = lax.dot_general(ql[i], cl[i], dims, preferred_element_type=jnp.float32)
        s = s + lax.dot_general(qr[i], cr[i], dims, preferred_element_type=jnp.float32)
        s = s * score_scale
        live = lax.broadcasted_iota(jnp.int32, s.shape, 1) < len_ref[i]
        s = jnp.where(live, s, -1e30)
        top = jnp.max(s, axis=-1, keepdims=True)
        w = jnp.where(live, jnp.exp(s - top), 0.0)
        w = (w / jnp.sum(w, axis=-1, keepdims=True)).astype(jnp.bfloat16)
        attn[i] = jnp.dot(w, cl[i], preferred_element_type=jnp.float32).astype(jnp.bfloat16)

    def project(g, first):
        x = xs[g].reshape(total, chunk)
        at = pl.ds(pl.multiple_of(g * chunk, chunk), chunk)
        for e in range(local):
            for n, w in enumerate((wg, wu)):
                y = jnp.dot(x, w[e, at, :], preferred_element_type=jnp.float32)
                if first:
                    acc[2 * e + n] = y
                else:
                    acc[2 * e + n] = acc[2 * e + n] + y

    for u in range(parts + 1):
        gather_z(u)
    for copy in loads:
        copy.wait()
    attend(0)
    attended = 1
    attn_copy = None
    waited = False
    for t in range(parts + 4):
        if t <= parts:
            gather_xy(t)
        if 0 <= t - 1 <= parts:
            gather_diag(t - 1)
        if 0 <= t - 2 <= parts:
            gather_done(t - 2)
        while attended < rows and (attended <= t + 1 or t >= 2):
            attend(attended)
            attended += 1
            if t < parts + 1:
                break
        if attended == rows and attn_copy is None:
            attn_copy = pltpu.make_async_copy(attn, attn_hbm, load_sem.at[4])
            attn_copy.start()
        if not waited and t >= 3:
            for copy in weights:
                copy.wait()
            waited = True
        if 1 <= t - 2 <= parts:
            k = t - 3
            if waited:
                project(c * parts + k, k == 0)
        if 1 <= t - 3 <= parts:
            k = t - 4
            g = other * parts + k
            arrived(xs.at[g], gs_s.at[k], gs_r.at[k], sib_id)
            project(g, False)

    col = lax.broadcasted_iota(jnp.int32, (total, LANES), 1)
    routes = table[...].reshape(total, LANES).astype(jnp.float32)
    for e in range(local):
        w = jnp.sum(jnp.where(col == ep * local + e, routes, 0.0), axis=-1, keepdims=True)
        gate, up = acc[2 * e], acc[2 * e + 1]
        hid[:, e * ff : (e + 1) * ff] = (gate / (1.0 + jnp.exp(-gate)) * up * w).astype(
            jnp.bfloat16
        )

    def f32(v):
        return v.astype(jnp.float32)

    def down(k):
        for own in (False, True):
            g = (c if own else other) * parts + k
            at = pl.ds(pl.multiple_of(g * chunk, chunk), chunk)
            y = jnp.dot(hid[...], wd[:, at], preferred_element_type=jnp.float32)
            if own:
                yown[k] = y.reshape(yown.shape[1:])
            else:
                ysib[k] = y.astype(jnp.bfloat16).reshape(ysib.shape[1:])
                send(ysib.at[k], r1.at[k], r1_s.at[k], r1_r.at[k], sib_id)

    def reduce_pair(k):
        arrived(r1.at[k], r1_s.at[k], r1_r.at[k], sib_id)
        zb[k] = (yown[k] + f32(r1[k])).astype(jnp.bfloat16)
        send(zb.at[k, dg, pl.ds(0, 2)], ra.at[k, 0], ra_s.at[k, 0], ra_r.at[k, 0], x_id)
        send(zb.at[k, dg, pl.ds(2, 2)], ra.at[k, 1], ra_s.at[k, 1], ra_r.at[k, 1], y_id)

    def reduce_diag(k):
        arrived(ra.at[k, 0], ra_s.at[k, 0], ra_r.at[k, 0], x_id)
        zb[k, yn, 0:2] = (f32(zb[k, yn, 0:2]) + f32(ra[k, 0])).astype(jnp.bfloat16)
        send(zb.at[k, yn], rb.at[k, 1], rb_s.at[k, 1], rb_r.at[k, 1], y_id)
        arrived(ra.at[k, 1], ra_s.at[k, 1], ra_r.at[k, 1], y_id)
        zb[k, xn, 2:4] = (f32(zb[k, xn, 2:4]) + f32(ra[k, 1])).astype(jnp.bfloat16)
        send(zb.at[k, xn], rb.at[k, 0], rb_s.at[k, 0], rb_r.at[k, 0], x_id)

    def reduce_xy(k):
        arrived(rb.at[k, 1], rb_s.at[k, 1], rb_r.at[k, 1], y_id)
        arrived(rb.at[k, 0], rb_s.at[k, 0], rb_r.at[k, 0], x_id)
        zb[k, rep] = (f32(zb[k, rep]) + f32(rb[k, 0]) + f32(rb[k, 1])).astype(jnp.bfloat16)
        for d in (1, 2, 3):
            send(
                zb.at[k, rep, (z + d) % 4], rc.at[k, d - 1],
                rc_s.at[k, d - 1], rc_r.at[k, d - 1], z_id(d),
            )

    def reduce_z(k):
        s = f32(zb[k, rep, z])
        for d in (1, 2, 3):
            arrived(rc.at[k, d - 1], rc_s.at[k, d - 1], rc_r.at[k, d - 1], z_id(4 - d))
            s = s + f32(rc[k, d - 1])
        fin[k] = s.reshape(2, rows, chunk)
        send(fin.at[k, other], fin_in.at[k], fin_s.at[k], fin_r.at[k], sib_id)

    def finish(k):
        arrived(fin_in.at[k], fin_s.at[k], fin_r.at[k], sib_id)
        mine, theirs = fin[k, c], fin_in[k]
        for h in range(2):
            at = slice(h * half + k * chunk, h * half + (k + 1) * chunk)
            out_ref[:, at] = (
                f32(stream_ref[:, at]) + jnp.where(c == h, mine, theirs)
            ).astype(jnp.bfloat16)

    stages = [down, reduce_pair, reduce_diag, reduce_xy, reduce_z, finish]
    for t in range(parts + len(stages) - 1):
        for n, stage in enumerate(stages):
            if 0 <= t - n < parts:
                stage(t - n)
    for copy in sent:
        copy.wait_send()
    attn_copy.wait()


def fused(parts, *args):
    (q_latent, q_rope, cache_latent, cache_rope, cache_len, stream, norm_gain,
     expert_ids, route_weights, w_gate, w_up, w_down) = args
    rows, width = stream.shape
    half = width // 2
    chunk = half // parts
    local, _, ff = w_gate.shape
    total = 32 * rows
    pair = 2 * rows
    bf, fl = jnp.bfloat16, jnp.float32
    vm, dma = pltpu.VMEM, pltpu.SemaphoreType.DMA
    space = lambda s: pl.BlockSpec(memory_space=s)
    in_specs = [space(pl.ANY)] * 4 + [space(pltpu.SMEM)] + [space(vm)] * 4 + [space(pl.ANY)] * 3
    scratch = [
        vm(q_latent.shape, bf), vm(q_rope.shape, bf), vm(cache_latent.shape, bf),
        vm(cache_rope.shape, bf), vm(q_latent.shape, bf),
        vm(w_gate.shape, bf), vm(w_up.shape, bf), vm((local * ff, width), bf),
        vm((2, rows, half + LANES), fl), vm((rows, half + LANES), fl), vm((rows, half + LANES), fl),
        vm((2 * parts, 4, 4, pair, chunk), bf), vm((4, 4, pair, LANES), bf),
        vm((2 * local, total, ff), fl), vm((total, local * ff), bf),
        vm((parts, 4, 4, pair, chunk), bf), vm((parts, 4, 4, pair, chunk), fl),
        vm((parts, 4, 4, pair, chunk), bf), vm((parts, 4, 4, pair, chunk), bf),
        vm((parts, 2, 2, pair, chunk), bf), vm((parts, 2, 4, pair, chunk), bf),
        vm((parts, 3, pair, chunk), bf), vm((parts, 2, rows, chunk), fl), vm((parts, rows, chunk), fl),
        dma((5,)), dma((3 * local,)), dma((2,)),
        dma((parts + 1, 3)), dma((parts + 1, 3)), dma((parts + 1, 2)), dma((parts + 1, 2)),
        dma((parts + 1, 2)), dma((parts + 1, 2)), dma((parts,)), dma((parts,)),
        dma((parts,)), dma((parts,)), dma((parts, 2)), dma((parts, 2)),
        dma((parts, 2)), dma((parts, 2)), dma((parts, 3)), dma((parts, 3)),
        dma((parts,)), dma((parts,)),
    ]
    return pl.pallas_call(
        functools.partial(fused_kernel, parts),
        out_shape=(
            jax.ShapeDtypeStruct(q_latent.shape, bf),
            jax.ShapeDtypeStruct(stream.shape, bf),
        ),
        in_specs=in_specs,
        out_specs=(space(pl.ANY), space(vm)),
        scratch_shapes=scratch,
        compiler_params=pltpu.CompilerParams(
            collective_id=0, has_side_effects=True, vmem_limit_bytes=58 * 2**20
        ),
    )(q_latent, q_rope, cache_latent, cache_rope, cache_len, stream,
      norm_gain.reshape(1, width), expert_ids, route_weights, w_gate, w_up, w_down)


def solution(mesh):
    placed = (
        P(("rep", "ep"), None, None),
        P(("rep", "ep"), None, None),
        P(("rep", "ep"), None, None),
        P(("rep", "ep"), None, None),
        P(("rep", "ep")),
        P(("rep", "ep"), None),
        P(),
        P(("rep", "ep"), None),
        P(("rep", "ep"), None),
        P("ep", None, "rep"),
        P("ep", None, "rep"),
        P("ep", "rep", None),
    )
    small = mesh.shape["rep"] == 4 and mesh.shape["ep"] == 8
    return jax.shard_map(
        functools.partial(fused, PARTS) if small else per_device,
        mesh=mesh,
        in_specs=placed,
        out_specs=(P(("rep", "ep"), None, None), P(("rep", "ep"), None)),
        check_vma=False,
    )
```

```python
import functools

import jax
import jax.numpy as jnp
from jax import lax
from jax.experimental import pallas as pl
from jax.experimental.pallas import tpu as pltpu
from jax.sharding import PartitionSpec as P

MESH = pl.DeviceIdType.MESH
LANES = 128
PARTS = 4

score_scale = 192.0 ** (-0.5)
norm_eps = 1e-06


def slot_ranks(routes):
    order = jnp.arange(routes.shape[0], dtype=jnp.int32)
    earlier = (routes[:, None] == routes[None, :]) & (order[None, :] < order[:, None])
    return jnp.sum(earlier.astype(jnp.int32), axis=-1)


def fill_slots(features, slot_index, row_index, slot_total):
    sources = jnp.zeros((slot_total,), jnp.int32).at[slot_index].set(row_index)
    filled = jnp.zeros((slot_total,), features.dtype).at[slot_index].set(1)
    return features[sources] * filled[:, None]


def expert_block(tokens_in, gate_part, up_part, down_part):
    gate_act = jnp.dot(tokens_in, gate_part, preferred_element_type=jnp.float32)
    up_act = jnp.dot(tokens_in, up_part, preferred_element_type=jnp.float32)
    hidden = (jax.nn.silu(gate_act) * up_act).astype(jnp.bfloat16)
    return jnp.dot(hidden, down_part, preferred_element_type=jnp.float32).astype(jnp.bfloat16)


def per_device(
    q_latent,
    q_rope,
    cache_latent,
    cache_rope,
    cache_len,
    stream,
    norm_gain,
    expert_ids,
    route_weights,
    w_gate,
    w_up,
    w_down,
):
    ep_count = lax.axis_size("ep")
    row_count, feature_dim = stream.shape
    local_count = w_gate.shape[0]
    top_count = expert_ids.shape[1]
    expert_total = local_count * ep_count
    capacity = max(2, 2 * row_count * top_count // expert_total)
    stream_f = stream.astype(jnp.float32)
    normed = (
        stream_f
        * lax.rsqrt(jnp.mean(stream_f * stream_f, axis=-1, keepdims=True) + norm_eps)
        * norm_gain
    ).astype(jnp.bfloat16)
    flat_routes = expert_ids.reshape(-1)
    rank_in = slot_ranks(flat_routes)
    expert_slot = flat_routes % local_count * ep_count + flat_routes // local_count
    slot_index = expert_slot * capacity + rank_in
    row_index = jnp.arange(row_count * top_count, dtype=jnp.int32) // top_count
    slot_total = expert_total * capacity
    outgoing = fill_slots(normed, slot_index, row_index, slot_total).reshape(
        local_count, ep_count, capacity, feature_dim
    )
    incoming = lax.all_to_all(outgoing, "ep", split_axis=1, concat_axis=1, tiled=True)
    incoming = incoming.reshape(local_count, ep_count * capacity, feature_dim)
    scores = (
        jnp.einsum("ihl,itl->iht", q_latent, cache_latent, preferred_element_type=jnp.float32)
        + jnp.einsum("ihr,itr->iht", q_rope, cache_rope, preferred_element_type=jnp.float32)
    ) * score_scale
    valid_mask = (
        jnp.arange(cache_latent.shape[1], dtype=jnp.int32)[None, None, :] < cache_len[:, None, None]
    )
    scores = jnp.where(valid_mask, scores, -1e30)
    top_score = jnp.max(scores, axis=-1, keepdims=True)
    exponent = jnp.where(valid_mask, jnp.exp(scores - top_score), 0.0)
    attn_weights = (exponent / jnp.sum(exponent, axis=-1, keepdims=True)).astype(jnp.bfloat16)
    attn_latent = jnp.einsum(
        "iht,itl->ihl", attn_weights, cache_latent, preferred_element_type=jnp.float32
    ).astype(jnp.bfloat16)
    everyone = lax.all_gather(incoming, "rep", axis=1, tiled=True)
    partials = jax.vmap(expert_block)(everyone, w_gate, w_up, w_down)
    partials = lax.optimization_barrier(partials)
    summed = lax.psum_scatter(
        partials.astype(jnp.float32).astype(jnp.bfloat16), "rep", scatter_dimension=1, tiled=True
    ).astype(jnp.float32)
    returned = lax.all_to_all(
        summed.reshape(local_count, ep_count, capacity, feature_dim).astype(jnp.bfloat16),
        "ep",
        split_axis=1,
        concat_axis=1,
        tiled=True,
    ).astype(jnp.float32)
    picked = returned.reshape(slot_total, feature_dim)[slot_index].reshape(
        row_count, top_count, feature_dim
    )
    expert_sum = jnp.einsum(
        "rk,rkd->rd", route_weights.astype(jnp.float32), picked, precision=lax.Precision.HIGHEST
    )
    layer_out = (stream_f + expert_sum).astype(jnp.bfloat16)
    return (attn_latent, layer_out)


def fused_kernel(
    parts,
    ql_hbm, qr_hbm, cl_hbm, cr_hbm, len_ref, stream_ref, gain_ref, ids_ref, rw_ref,
    wg_hbm, wu_hbm, wd_hbm,
    attn_hbm, out_ref,
    ql, qr, cl, cr, attn, wg, wu, wd,
    nrm, swap_out, swap_in, xs, table, acc, hid,
    ysib, yown, r1, zb, ra, rb, rc, fin, fin_in,
    load_sem, w_sem, swap_sem, go_s, go_r,
    gz_s, gz_r, gc_s, gc_r, gf_s, gf_r, gs_s, gs_r,
    r1_s, r1_r, ra_s, ra_r, rb_s, rb_r, rc_s, rc_r, fin_s, fin_r,
):
    rep = lax.axis_index("rep")
    ep = lax.axis_index("ep")
    z, c = ep // 2, ep % 2
    other = 1 - c
    xn = rep + 1 - 2 * (rep % 2)
    yn = (rep + 2) % 4
    dg = 3 - rep
    sib_id = (rep, z * 2 + other)
    x_id, y_id = (xn, ep), (yn, ep)

    def z_id(d):
        return (rep, ((z + d) % 4) * 2 + c)

    partners = [sib_id, x_id, y_id, z_id(1), z_id(2), z_id(3)]
    rows, width = stream_ref.shape
    half = width // 2
    chunk = half // parts
    local = wg.shape[0]
    ff = wg.shape[2]
    total = 32 * rows

    barrier = pltpu.get_barrier_semaphore()
    for p in partners:
        pl.semaphore_signal(barrier, inc=1, device_id=p, device_id_type=MESH)

    loads = []
    for n, (a, b) in enumerate([(ql_hbm, ql), (cl_hbm, cl), (qr_hbm, qr), (cr_hbm, cr)]):
        loads.append(pltpu.make_async_copy(a, b, load_sem.at[n]))
    weights = []
    for e in range(local):
        weights.append(pltpu.make_async_copy(wg_hbm.at[e], wg.at[e], w_sem.at[3 * e]))
        weights.append(pltpu.make_async_copy(wu_hbm.at[e], wu.at[e], w_sem.at[3 * e + 1]))
        weights.append(
            pltpu.make_async_copy(wd_hbm.at[e], wd.at[pl.ds(e * ff, ff)], w_sem.at[3 * e + 2])
        )
    for copy in loads + weights:
        copy.start()

    stream_f = stream_ref[...].astype(jnp.float32)
    scale = lax.rsqrt(jnp.mean(stream_f * stream_f, axis=-1, keepdims=True) + norm_eps)
    normed = (stream_f * scale * gain_ref[...]).astype(jnp.bfloat16).astype(jnp.float32)
    for h in range(2):
        nrm[h, :, :half] = normed[:, h * half : (h + 1) * half]
    lane = lax.broadcasted_iota(jnp.int32, (rows, LANES), 1)
    dense = jnp.zeros((rows, LANES), jnp.float32)
    ids, rw = ids_ref[...], rw_ref[...].astype(jnp.float32)
    for k in range(ids.shape[1]):
        dense = dense + jnp.where(lane == ids[:, k : k + 1], rw[:, k : k + 1], 0.0)
    for h in range(2):
        nrm[h, :, half:] = dense
    swap_out[...] = nrm[other]
    pl.semaphore_wait(barrier, len(partners))

    sent = []

    def send(src, dst, send_sem, recv_sem, to):
        copy = pltpu.make_async_remote_copy(
            src_ref=src, dst_ref=dst, send_sem=send_sem, recv_sem=recv_sem,
            device_id=to, device_id_type=MESH,
        )
        copy.start()
        sent.append(copy)

    def arrived(dst, send_sem, recv_sem, to):
        pltpu.make_async_remote_copy(
            src_ref=dst, dst_ref=dst, send_sem=send_sem, recv_sem=recv_sem,
            device_id=to, device_id_type=MESH,
        ).wait_recv()

    send(swap_out, swap_in, swap_sem.at[0], swap_sem.at[1], sib_id)
    arrived(swap_in, swap_sem.at[0], swap_sem.at[1], sib_id)
    mine, theirs = nrm[c], swap_in[...]
    both = jnp.where(
        c == 0,
        jnp.concatenate([mine, theirs], axis=0),
        jnp.concatenate([theirs, mine], axis=0),
    ).astype(jnp.bfloat16)
    table[rep, z] = both[:, half:]
    units = []
    for k in range(parts):
        xs[c * parts + k, rep, z] = both[:, k * chunk : (k + 1) * chunk]
        units.append(xs.at[c * parts + k])
    units.append(table)
    own = pl.ds(c * parts, parts)
    for n, to in enumerate((x_id, y_id)):
        send(xs.at[own, rep, z], xs.at[own, rep, z], go_s.at[n], go_r.at[n], to)
        blk = table.at[rep, z]
        send(blk, blk, go_s.at[n + 2], go_r.at[n + 2], to)

    def gather_z(u):
        for d in (1, 2, 3):
            blk = units[u].at[rep, z]
            send(blk, blk, gz_s.at[u, d - 1], gz_r.at[u, d - 1], z_id(d))

    def gather_xy(u):
        for d in (1, 2, 3):
            blk = units[u].at[rep, (z + 4 - d) % 4]
            arrived(blk, gz_s.at[u, d - 1], gz_r.at[u, d - 1], z_id(4 - d))
            send(blk, blk, gc_s.at[u, d - 1], gc_r.at[u, d - 1], x_id)
            send(blk, blk, gc_s.at[u, d + 2], gc_r.at[u, d + 2], y_id)

    def column_in(u, n, src, to):
        if u == 0:
            arrived(xs.at[own, src, z], go_s.at[n], go_r.at[n], to)
        if u == parts:
            arrived(table.at[src, z], go_s.at[n + 2], go_r.at[n + 2], to)
        for d in (1, 2, 3):
            m = d - 1 + 3 * n
            arrived(units[u].at[src, (z + 4 - d) % 4], gc_s.at[u, m], gc_r.at[u, m], to)

    def gather_diag(u):
        column_in(u, 0, xn, x_id)
        low = units[u].at[xn, pl.ds(0, 2)]
        send(low, low, gf_s.at[u, 0], gf_r.at[u, 0], y_id)
        column_in(u, 1, yn, y_id)
        high = units[u].at[yn, pl.ds(2, 2)]
        send(high, high, gf_s.at[u, 1], gf_r.at[u, 1], x_id)

    def gather_done(u):
        arrived(units[u].at[dg, pl.ds(0, 2)], gf_s.at[u, 0], gf_r.at[u, 0], y_id)
        arrived(units[u].at[dg, pl.ds(2, 2)], gf_s.at[u, 1], gf_r.at[u, 1], x_id)
        if u < parts:
            send(units[u], units[u], gs_s.at[u], gs_r.at[u], sib_id)

    def attend(i):
        dims = (((1,), (1,)), ((), ()))
        s = lax.dot_general(ql[i], cl[i], dims, preferred_element_type=jnp.float32)
        s = s + lax.dot_general(
            qr[i], cr[i], (((0,), (0,)), ((), ())), preferred_element_type=jnp.float32
        )
        s = s * score_scale
        live = lax.broadcasted_iota(jnp.int32, s.shape, 1) < len_ref[i]
        s = jnp.where(live, s, -1e30)
        top = jnp.max(s, axis=-1, keepdims=True)
        w = jnp.where(live, jnp.exp(s - top), 0.0)
        w = (w / jnp.sum(w, axis=-1, keepdims=True)).astype(jnp.bfloat16)
        attn[i] = jnp.dot(w, cl[i], preferred_element_type=jnp.float32).astype(jnp.bfloat16)

    def project(g, first):
        x = xs[g].reshape(total, chunk)
        at = pl.ds(pl.multiple_of(g * chunk, chunk), chunk)
        for e in range(local):
            for n, w in enumerate((wg, wu)):
                y = jnp.dot(x, w[e, at, :], preferred_element_type=jnp.float32)
                if first:
                    acc[2 * e + n] = y
                else:
                    acc[2 * e + n] = acc[2 * e + n] + y

    def step(stage, u):
        if 0 <= u < parts:
            stage(u)
        if u == 0:
            stage(parts)

    for u in range(parts):
        step(gather_z, u)
    for copy in loads:
        copy.wait()
    attend(0)
    step(gather_xy, 0)
    step(gather_xy, 1)
    attended = 1
    for t in range(parts + 3):
        step(gather_xy, t + 2)
        step(gather_diag, t)
        step(gather_done, t - 1)
        while attended < rows and (attended <= t + 1 or t == parts + 2):
            attend(attended)
            attended += 1
        if t == parts + 2:
            attn_copy = pltpu.make_async_copy(attn, attn_hbm, load_sem.at[4])
            attn_copy.start()
        if t == 1:
            for copy in weights:
                copy.wait()
        if 0 <= t - 1 < parts:
            project(c * parts + t - 1, t == 1)
        if 0 <= t - 2 < parts:
            k = t - 2
            g = other * parts + k
            arrived(xs.at[g], gs_s.at[k], gs_r.at[k], sib_id)
            project(g, False)

    col = lax.broadcasted_iota(jnp.int32, (total, LANES), 1)
    routes = table[...].reshape(total, LANES).astype(jnp.float32)
    for e in range(local):
        w = jnp.sum(jnp.where(col == ep * local + e, routes, 0.0), axis=-1, keepdims=True)
        gate, up = acc[2 * e], acc[2 * e + 1]
        hid[:, e * ff : (e + 1) * ff] = (gate / (1.0 + jnp.exp(-gate)) * up * w).astype(
            jnp.bfloat16
        )

    def f32(v):
        return v.astype(jnp.float32)

    def down(k):
        for own in (False, True):
            g = (c if own else other) * parts + k
            at = pl.ds(pl.multiple_of(g * chunk, chunk), chunk)
            y = jnp.dot(hid[...], wd[:, at], preferred_element_type=jnp.float32)
            if own:
                yown[k] = y.reshape(yown.shape[1:])
            else:
                ysib[k] = y.astype(jnp.bfloat16).reshape(ysib.shape[1:])
                send(ysib.at[k], r1.at[k], r1_s.at[k], r1_r.at[k], sib_id)

    def reduce_pair(k):
        arrived(r1.at[k], r1_s.at[k], r1_r.at[k], sib_id)
        zb[k] = (yown[k] + f32(r1[k])).astype(jnp.bfloat16)
        send(zb.at[k, dg, pl.ds(0, 2)], ra.at[k, 0], ra_s.at[k, 0], ra_r.at[k, 0], x_id)
        send(zb.at[k, dg, pl.ds(2, 2)], ra.at[k, 1], ra_s.at[k, 1], ra_r.at[k, 1], y_id)

    def reduce_diag(k):
        arrived(ra.at[k, 0], ra_s.at[k, 0], ra_r.at[k, 0], x_id)
        zb[k, yn, 0:2] = (f32(zb[k, yn, 0:2]) + f32(ra[k, 0])).astype(jnp.bfloat16)
        send(zb.at[k, yn], rb.at[k, 1], rb_s.at[k, 1], rb_r.at[k, 1], y_id)
        arrived(ra.at[k, 1], ra_s.at[k, 1], ra_r.at[k, 1], y_id)
        zb[k, xn, 2:4] = (f32(zb[k, xn, 2:4]) + f32(ra[k, 1])).astype(jnp.bfloat16)
        send(zb.at[k, xn], rb.at[k, 0], rb_s.at[k, 0], rb_r.at[k, 0], x_id)

    def reduce_xy(k):
        arrived(rb.at[k, 1], rb_s.at[k, 1], rb_r.at[k, 1], y_id)
        arrived(rb.at[k, 0], rb_s.at[k, 0], rb_r.at[k, 0], x_id)
        zb[k, rep] = (f32(zb[k, rep]) + f32(rb[k, 0]) + f32(rb[k, 1])).astype(jnp.bfloat16)
        for d in (1, 2, 3):
            send(
                zb.at[k, rep, (z + d) % 4], rc.at[k, d - 1],
                rc_s.at[k, d - 1], rc_r.at[k, d - 1], z_id(d),
            )

    def reduce_z(k):
        s = f32(zb[k, rep, z])
        for d in (1, 2, 3):
            arrived(rc.at[k, d - 1], rc_s.at[k, d - 1], rc_r.at[k, d - 1], z_id(4 - d))
            s = s + f32(rc[k, d - 1])
        fin[k] = s.reshape(2, rows, chunk)
        send(fin.at[k, other], fin_in.at[k], fin_s.at[k], fin_r.at[k], sib_id)

    def finish(k):
        arrived(fin_in.at[k], fin_s.at[k], fin_r.at[k], sib_id)
        mine, theirs = fin[k, c], fin_in[k]
        for h in range(2):
            at = slice(h * half + k * chunk, h * half + (k + 1) * chunk)
            out_ref[:, at] = (
                f32(stream_ref[:, at]) + jnp.where(c == h, mine, theirs)
            ).astype(jnp.bfloat16)

    stages = [down, reduce_pair, reduce_diag, reduce_xy, reduce_z, finish]
    for t in range(parts + len(stages) - 1):
        for n, stage in enumerate(stages):
            if 0 <= t - n < parts:
                stage(t - n)
    for copy in sent:
        copy.wait_send()
    attn_copy.wait()


def fused(parts, *args):
    (q_latent, q_rope, cache_latent, cache_rope, cache_len, stream, norm_gain,
     expert_ids, route_weights, w_gate, w_up, w_down) = args
    q_rope, cache_rope = q_rope.swapaxes(1, 2), cache_rope.swapaxes(1, 2)
    rows, width = stream.shape
    half = width // 2
    chunk = half // parts
    local, _, ff = w_gate.shape
    total = 32 * rows
    pair = 2 * rows
    bf, fl = jnp.bfloat16, jnp.float32
    vm, dma = pltpu.VMEM, pltpu.SemaphoreType.DMA
    space = lambda s: pl.BlockSpec(memory_space=s)
    in_specs = [space(pl.ANY)] * 4 + [space(pltpu.SMEM)] + [space(vm)] * 4 + [space(pl.ANY)] * 3
    scratch = [
        vm(q_latent.shape, bf), vm(q_rope.shape, bf), vm(cache_latent.shape, bf),
        vm(cache_rope.shape, bf), vm(q_latent.shape, bf),
        vm(w_gate.shape, bf), vm(w_up.shape, bf), vm((local * ff, width), bf),
        vm((2, rows, half + LANES), fl), vm((rows, half + LANES), fl), vm((rows, half + LANES), fl),
        vm((2 * parts, 4, 4, pair, chunk), bf), vm((4, 4, pair, LANES), bf),
        vm((2 * local, total, ff), fl), vm((total, local * ff), bf),
        vm((parts, 4, 4, pair, chunk), bf), vm((parts, 4, 4, pair, chunk), fl),
        vm((parts, 4, 4, pair, chunk), bf), vm((parts, 4, 4, pair, chunk), bf),
        vm((parts, 2, 2, pair, chunk), bf), vm((parts, 2, 4, pair, chunk), bf),
        vm((parts, 3, pair, chunk), bf), vm((parts, 2, rows, chunk), fl), vm((parts, rows, chunk), fl),
        dma((5,)), dma((3 * local,)), dma((2,)), dma((4,)), dma((4,)),
        dma((parts + 1, 3)), dma((parts + 1, 3)), dma((parts + 1, 6)), dma((parts + 1, 6)),
        dma((parts + 1, 2)), dma((parts + 1, 2)), dma((parts,)), dma((parts,)),
        dma((parts,)), dma((parts,)), dma((parts, 2)), dma((parts, 2)),
        dma((parts, 2)), dma((parts, 2)), dma((parts, 3)), dma((parts, 3)),
        dma((parts,)), dma((parts,)),
    ]
    return pl.pallas_call(
        functools.partial(fused_kernel, parts),
        out_shape=(
            jax.ShapeDtypeStruct(q_latent.shape, bf),
            jax.ShapeDtypeStruct(stream.shape, bf),
        ),
        in_specs=in_specs,
        out_specs=(space(pl.ANY), space(vm)),
        scratch_shapes=scratch,
        compiler_params=pltpu.CompilerParams(
            collective_id=0, has_side_effects=True, vmem_limit_bytes=58 * 2**20
        ),
    )(q_latent, q_rope, cache_latent, cache_rope, cache_len, stream,
      norm_gain.reshape(1, width), expert_ids, route_weights, w_gate, w_up, w_down)


def solution(mesh):
    placed = (
        P(("rep", "ep"), None, None),
        P(("rep", "ep"), None, None),
        P(("rep", "ep"), None, None),
        P(("rep", "ep"), None, None),
        P(("rep", "ep")),
        P(("rep", "ep"), None),
        P(),
        P(("rep", "ep"), None),
        P(("rep", "ep"), None),
        P("ep", None, "rep"),
        P("ep", None, "rep"),
        P("ep", "rep", None),
    )
    small = mesh.shape["rep"] == 4 and mesh.shape["ep"] == 8
    return jax.shard_map(
        functools.partial(fused, PARTS) if small else per_device,
        mesh=mesh,
        in_specs=placed,
        out_specs=(P(("rep", "ep"), None, None), P(("rep", "ep"), None)),
        check_vma=False,
    )
```
